256 devices in a mesh: slab: 16 (over y, z_lo, core), spec: 16 (over x, z_hi).
Axes of the slice: x: 4, y: 4, z: 8 (z_hi: 4, z_lo: 2; z = z_hi * 2 + z_lo), core: 2. Of those that a mesh axis runs over, the one named last changes fastest.
Arguments:
- concentration: bfloat16 [256, 128, 16, 128], P('spec', 'slab'), may hold values from 0.049804688 to 2
- inhibit: bfloat16 [256, 256], replicated, may hold values from 0 to 0.015625
- priming: bfloat16 [256, 256], replicated, may hold values from 0 to 0.0077819824
- produce: bfloat16 [256, 256], replicated, may hold values from 0 to 0.0059814453
- max_rate: float32 [256], replicated, may hold values from 0.05 to 1
- half_saturation: float32 [256], replicated, may hold values from 0.2 to 2
- exudate: float32 [256], replicated, may hold values from 0.01 to 0.5
- sorption_capacity: float32 [8, 256], replicated, may hold values from 1 to 40
- sorption_affinity: float32 [8, 256], replicated, may hold values from 0.005 to 0.05
- tortuosity: float32 [8], replicated, may hold values from 0.2 to 1
- diffusivity: float32 [256], P('spec'), may hold values from 0.01 to 0.08
- velocity: float32 [128, 16, 128], P('slab'), may hold values from 0.1 to 0.5
- material: int32 [128, 16, 128], P('slab'), may hold values from 0 to 7
- root_mask: int32 [128, 16, 128], P('slab'), may hold values 0 or 1
Outputs:
- concentration_out: bfloat16 [256, 128, 16, 128], P('spec', 'slab')
The draws below stay inside these ranges and needn't reach their ends.
All inputs are finite; a program needn't handle non-finite values. No bound on the sum of `root_mask` on one device may be relied on, other than what follows from the above.
Results may differ from the reference program's by a relative error of at most 0.0007.
The reference program's roundings to bfloat16 on the way (of `consumed` and `renewed`) count: a program that leaves them out, or rounds other values in their place, can miss the bound.
Values may be sent and summed in bfloat16 or wider, within the bound.
A program may use at most 64 MiB of HBM per device.

```python
import math
import jax
import jax.numpy as jnp
from jax import lax

S = 256
M = 8
NY = 16
NX = 128
SUB = 4
STEPS = 2
NZ = 128


def plant(array, stream_key, least, high):
    index_at = [jax.random.randint(jax.random.fold_in(stream_key, axis), (), 0, length) for axis, length in enumerate(array.shape)]
    widest = array.shape.index(max(array.shape))
    neighbour = index_at[:widest] + [(index_at[widest] + 1) % array.shape[widest]] + index_at[widest + 1:]
    return array.at[tuple(index_at)].set(least).at[tuple(neighbour)].set(high)


def level_of(stream_key, extent, pieces, low, high):
    gain, own = 1.0, jax.random.fold_in(stream_key, 6)
    for position, parts in pieces:
        heights = jnp.exp(jax.random.uniform(jax.random.fold_in(own, position), (parts,), jnp.float32, low / len(pieces), high / len(pieces)))
        gain = gain * jnp.repeat(heights, extent[position] // parts).reshape([-1 if axis == position else 1 for axis in range(len(extent))])
    return gain


def setup_inputs(seed: int = 0) -> dict:
    splits = jax.random.split(jax.random.key(seed), 15)
    return {
        "concentration": jnp.clip(jnp.exp(math.log(2.0) - 3.6927934 * jax.random.uniform(splits[0], (S, NZ, NY, NX), jnp.float32) ** level_of(splits[0], (S, NZ, NY, NX), ((0, 16), (1, 16)), -0.2, 0.2)), 0.049804688, 2.0).astype(jnp.bfloat16),
        "inhibit": jnp.clip(jax.random.uniform(splits[1], (S, S), jnp.float32, 0.0, 0.015625), 0.0, 0.015625).astype(jnp.bfloat16),
        "priming": jnp.clip(jax.random.uniform(splits[2], (S, S), jnp.float32, 0.0, 0.0077819824), 0.0, 0.0077819824).astype(jnp.bfloat16),
        "produce": jnp.clip(jax.random.uniform(splits[3], (S, S), jnp.float32, 0.0, 0.0059814453), 0.0, 0.0059814453).astype(jnp.bfloat16),
        "max_rate": jnp.clip(jnp.exp(jax.random.uniform(splits[4], (S,), jnp.float32, math.log(0.05), math.log(1.0))), 0.05, 1.0),
        "half_saturation": jnp.clip(jnp.exp(jax.random.uniform(splits[5], (S,), jnp.float32, math.log(0.2), math.log(2.0))), 0.2, 2.0),
        "exudate": jnp.clip(jnp.exp(jax.random.uniform(splits[6], (S,), jnp.float32, math.log(0.01), math.log(0.5))), 0.01, 0.5),
        "sorption_capacity": jnp.clip(jnp.exp(jax.random.uniform(splits[7], (M, S), jnp.float32, math.log(1.0), math.log(40.0))), 1.0, 40.0),
        "sorption_affinity": jnp.clip(jnp.exp(jax.random.uniform(splits[8], (M, S), jnp.float32, math.log(0.005), math.log(0.05))), 0.005, 0.05),
        "tortuosity": jnp.clip(jnp.exp(jax.random.uniform(splits[9], (M,), jnp.float32, math.log(0.2), math.log(1.0))), 0.2, 1.0),
        "diffusivity": jnp.clip(0.01 + 0.07 * jax.random.uniform(splits[10], (S,), jnp.float32) ** level_of(splits[10], (S,), ((0, 16),), -0.2, 0.2), 0.01, 0.08),
        "velocity": jnp.clip(0.1 + 0.4 * jax.random.uniform(splits[11], (NZ, NY, NX), jnp.float32) ** level_of(splits[11], (NZ, NY, NX), ((0, 16),), -0.2, 0.2), 0.1, 0.5),
        "material": plant(jax.random.randint(splits[12], (NZ, NY, NX), 0, M), jax.random.fold_in(splits[12], 1), 0, M - 1).astype(jnp.int32),
        "root_mask": plant((jax.random.randint(splits[13], (NZ, NY, NX), 0, 8) < 1).astype(jnp.int32), jax.random.fold_in(splits[13], 1), 0, 1),
    }


def pick_by_material(values_table, labels, trailing):
    summed = None
    for material_id in range(values_table.shape[0]):
        entry = values_table[material_id].reshape(values_table.shape[1:] + (1,) * trailing)
        term = jnp.where(labels == material_id, entry, jnp.zeros((), jnp.float32))
        summed = term if summed is None else summed + term
    return summed


def divergence(mobile_padded, flow_padded, tort_padded, spread_rate):
    face_z = 0.5 * (tort_padded[:-1] + tort_padded[1:])
    flux_z = flow_padded[:-1] * mobile_padded[..., :-1, :, :] - spread_rate * face_z * (mobile_padded[..., 1:, :, :] - mobile_padded[..., :-1, :, :])
    change = flux_z[..., :-1, :, :] - flux_z[..., 1:, :, :]
    mobile = mobile_padded[..., 1:-1, :, :]
    tortuous = tort_padded[1:-1]
    lead = [(0, 0)] * (mobile.ndim - 2)
    mobile_y = jnp.pad(mobile, lead + [(1, 1), (0, 0)])
    tort_y = jnp.pad(tortuous, ((0, 0), (1, 1), (0, 0)))
    face_y = 0.5 * (tort_y[:, :-1] + tort_y[:, 1:])
    flux_y = -spread_rate * face_y * (mobile_y[..., 1:, :] - mobile_y[..., :-1, :])
    change = change + flux_y[..., :-1, :] - flux_y[..., 1:, :]
    mobile_x = jnp.pad(mobile, lead + [(0, 0), (1, 1)])
    tort_x = jnp.pad(tortuous, ((0, 0), (0, 0), (1, 1)))
    face_x = 0.5 * (tort_x[:, :, :-1] + tort_x[:, :, 1:])
    flux_x = -spread_rate * face_x * (mobile_x[..., 1:] - mobile_x[..., :-1])
    change = change + flux_x[..., :-1] - flux_x[..., 1:]
    return change


def reaction(gathered, inhibit, priming, produce, max_rate, half_saturation, source_term, onehot, sorption_affinity):
    inhibition = jnp.dot(inhibit, gathered, preferred_element_type=jnp.float32)
    boost = jnp.dot(priming, gathered, preferred_element_type=jnp.float32)
    dissolved = gathered.astype(jnp.float32)
    rate_term = max_rate[:, None] * (1.0 + boost) / (half_saturation[:, None] + dissolved + inhibition)
    remaining = dissolved * jnp.exp(-rate_term)
    consumed = (dissolved - remaining).astype(jnp.bfloat16)
    reacted = remaining + jnp.dot(produce, consumed, preferred_element_type=jnp.float32) + source_term
    sorbed_sums = jnp.dot(sorption_affinity, reacted, precision=lax.Precision.HIGHEST)
    denominator = 1.0 + jnp.sum(onehot * sorbed_sums, axis=0)
    return reacted.astype(jnp.bfloat16), denominator


def reference(concentration, inhibit, priming, produce, max_rate, half_saturation, exudate, sorption_capacity, sorption_affinity, tortuosity, diffusivity, velocity, material, root_mask):
    tort_cells = pick_by_material(tortuosity, material, 0)
    flow_padded = jnp.pad(velocity, ((1, 1), (0, 0), (0, 0)))
    tort_padded = jnp.pad(tort_cells, ((1, 1), (0, 0), (0, 0)))
    uptake_table = sorption_capacity * sorption_affinity
    plane_labels = material.reshape(NZ, NY * NX)
    plane_roots = root_mask.reshape(NZ, NY * NX).astype(jnp.float32)
    for repeat in range(STEPS):
        planes = jnp.moveaxis(concentration, 1, 0).reshape(NZ, S, NY * NX)

        def react_plane(inputs):
            plane, labels, rooted = inputs
            onehot = (labels[None, :] == jnp.arange(M, dtype=jnp.int32)[:, None]).astype(jnp.float32)
            return reaction(plane, inhibit, priming, produce, max_rate, half_saturation, exudate[:, None] * rooted[None, :], onehot, sorption_affinity)

        renewed, denominator = lax.map(react_plane, (planes, plane_labels, plane_roots))
        renewed = jnp.moveaxis(renewed.reshape(NZ, S, NY, NX), 0, 1)
        denominator = denominator.reshape(NZ, NY, NX)

        def transport(inputs):
            species_field, uptake_column, spread_rate = inputs
            ratio = pick_by_material(uptake_column, material, 0)
            mobile_share = 1.0 / (1.0 + ratio / denominator)
            field = species_field.astype(jnp.float32)
            for substep in range(SUB):
                mobile_padded = jnp.pad(mobile_share * field, ((1, 1), (0, 0), (0, 0)))
                field = field + divergence(mobile_padded, flow_padded, tort_padded, spread_rate)
            return field.astype(jnp.bfloat16)

        concentration = lax.map(transport, (renewed, uptake_table.T, diffusivity))
    return concentration
```

```python
import functools

import jax
import jax.numpy as jnp
from jax import lax
from jax.experimental import pallas as pl
from jax.experimental.pallas import tpu as pltpu
from jax.sharding import PartitionSpec as P

SUB = 4
STEPS = 2
N = 16
NSLAB = 16
SP = 16
L = 8
E = L + 2 * SUB
Y = 16
X = 128
S = 256
M = 8
MESH = pl.DeviceIdType.MESH
f32 = jnp.float32
bf16 = jnp.bfloat16


def column(row):
    n = row.shape[1]
    eye = lax.broadcasted_iota(jnp.int32, (n, n), 0) == lax.broadcasted_iota(jnp.int32, (n, n), 1)
    return jnp.sum(jnp.where(eye, jnp.broadcast_to(row, (n, n)), 0.0), axis=1, keepdims=True)


def kernel(
    c_ref, inhibit_ref, priming_ref, produce_ref, vectors_ref, capacity_ref, affinity_ref, tort_ref, dif_ref,
    vel_ref, mat_ref, root_ref, out_ref,
    c32, send_a, recv_a, send_b, ren, den_send, den,
    matx, velx, tpad, cxr, cxl, fy, diag, cz, vz, ratio, uptake, mr, hs, ex, aff, root_b,
    fld, share, mob, outs,
    sem_as, sem_ar, sem_bs, sem_br, sem_ds, sem_dr, sem_hs, sem_hr, sem_gs, sem_gr, sem_cs, sem_cr,
):
    me = lax.axis_index("spec")
    slab = lax.axis_index("slab")
    below = lax.rem(slab + 1, NSLAB)
    above = lax.rem(slab + NSLAB - 1, NSLAB)

    barrier = pltpu.get_barrier_semaphore()

    @pl.loop(1, N)
    def _(d):
        pl.semaphore_signal(barrier, inc=1, device_id={"spec": lax.rem(me + d, N)}, device_id_type=MESH)

    for t in (below, above):
        pl.semaphore_signal(barrier, inc=1, device_id={"slab": t}, device_id_type=MESH)

    @pl.loop(0, SP)
    def _(s):
        for l in range(L):
            c32[pl.ds(s * L * Y + l * Y, Y), :] = c_ref[s, l].astype(f32)

    pl.semaphore_wait(barrier, N + 1)

    def copy_a(st, t, src):
        return pltpu.make_async_remote_copy(
            send_a.at[st, t], recv_a.at[st, me], sem_as.at[st, t], sem_ar.at[st, me],
            device_id={"spec": t}, device_id_type=MESH,
        )

    def wait_a(st, src):
        pltpu.make_async_remote_copy(
            send_a.at[st, src], recv_a.at[st, src], sem_as.at[st, src], sem_ar.at[st, src],
            device_id={"spec": src}, device_id_type=MESH,
        ).wait_recv()

    def wait_a_sent(st, t):
        copy_a(st, t, me).wait_send()

    def copy_b(st, t):
        return pltpu.make_async_remote_copy(
            send_b.at[st, t], ren.at[st, me, pl.ds(SUB, L)], sem_bs.at[st, t], sem_br.at[st, me],
            device_id={"spec": t}, device_id_type=MESH,
        )

    def copy_d(st, t):
        return pltpu.make_async_remote_copy(
            den_send.at[st], den.at[st, me, pl.ds(1, 2)], sem_ds.at[st, t], sem_dr.at[st, me],
            device_id={"spec": t}, device_id_type=MESH,
        )

    def wait_b(st, src):
        pltpu.make_async_remote_copy(
            send_b.at[st, src], ren.at[st, src, pl.ds(SUB, L)], sem_bs.at[st, src], sem_br.at[st, src],
            device_id={"spec": src}, device_id_type=MESH,
        ).wait_recv()

    def wait_d(st, src):
        pltpu.make_async_remote_copy(
            den_send.at[st], den.at[st, src, pl.ds(1, 2)], sem_ds.at[st, src], sem_dr.at[st, src],
            device_id={"spec": src}, device_id_type=MESH,
        ).wait_recv()

    def copies_h(st, y):
        down = pltpu.make_async_remote_copy(
            ren.at[st, y, pl.ds(L, SUB)], ren.at[st, y, pl.ds(0, SUB)], sem_hs.at[st, 0, y], sem_hr.at[st, 0, y],
            device_id={"slab": below}, device_id_type=MESH,
        )
        up = pltpu.make_async_remote_copy(
            ren.at[st, y, pl.ds(SUB, SUB)], ren.at[st, y, pl.ds(L + SUB, SUB)], sem_hs.at[st, 1, y], sem_hr.at[st, 1, y],
            device_id={"slab": above}, device_id_type=MESH,
        )
        return down, up

    def copies_g(st):
        down = pltpu.make_async_remote_copy(
            den.at[st, :, 2], den.at[st, :, 0], sem_gs.at[st, 0], sem_gr.at[st, 0],
            device_id={"slab": below}, device_id_type=MESH,
        )
        up = pltpu.make_async_remote_copy(
            den.at[st, :, 1], den.at[st, :, 3], sem_gs.at[st, 1], sem_gr.at[st, 1],
            device_id={"slab": above}, device_id_type=MESH,
        )
        return down, up

    def copies_c():
        out = []
        for i, (ref, dst) in enumerate(((mat_ref, matx), (vel_ref, velx))):
            out.append(pltpu.make_async_remote_copy(
                ref.at[pl.ds(L - SUB, SUB)], dst.at[pl.ds(0, SUB)], sem_cs.at[2 * i], sem_cr.at[2 * i],
                device_id={"slab": below}, device_id_type=MESH,
            ))
            out.append(pltpu.make_async_remote_copy(
                ref.at[pl.ds(0, SUB)], dst.at[pl.ds(L + SUB, SUB)], sem_cs.at[2 * i + 1], sem_cr.at[2 * i + 1],
                device_id={"slab": above}, device_id_type=MESH,
            ))
        return out

    @pl.loop(1, N + 1)
    def _(d):
        t = lax.rem(me + d, N)
        for l in range(L):
            send_a[0, t, l] = c32[pl.ds(l * Y + t, SP, stride=L * Y), :].astype(bf16)

        @pl.when(d < N)
        def _():
            copy_a(0, t, me).start()

    rims = copies_c()
    for cp in rims:
        cp.start()

    for l in range(L):
        matx[SUB + l] = mat_ref[l]
        velx[SUB + l] = vel_ref[l]
    for half in range(2):
        rows = pl.ds(half * 128, 128)
        for i, ref in enumerate((mr, hs, ex)):
            ref[rows, :] = jnp.broadcast_to(column(vectors_ref[2 * i + half : 2 * i + half + 1, :]), (128, X))
        for g in range(M):
            up = capacity_ref[g : g + 1, rows] * affinity_ref[g : g + 1, rows]
            uptake[g, rows, :] = jnp.broadcast_to(column(up), (128, X))
    a_hi = affinity_ref[...].astype(bf16)
    aff[0:M, :] = a_hi.astype(f32)
    aff[M : 2 * M, :] = affinity_ref[...] - a_hi.astype(f32)
    for l in range(L):
        root_b[l : l + 1, :] = root_ref[l, pl.ds(me, 1), :].astype(f32)
    dif = jnp.broadcast_to(column(dif_ref[...]), (SP, X))
    dif_h = (dif[0:8], dif[8:16])
    lane = lax.broadcasted_iota(jnp.int32, (Y, X), 1)
    zero_row = jnp.zeros((SP, X), f32)
    tpad[...] = jnp.zeros_like(tpad)
    for k in range(SUB):
        for e in range(E):
            mob[k, 0, e] = zero_row
            mob[k, Y + 1, e] = zero_row

    for cp in rims:
        cp.wait_recv()

    def inside(e):
        layer = slab * L + e - SUB
        return jnp.where((layer >= 0) & (layer < NSLAB * L), 1.0, 0.0).astype(f32)

    def tort_of(e):
        m = matx[e]
        t = jnp.zeros((Y, X), f32)
        for g in range(M):
            t = jnp.where(m == g, tort_ref[g], t)
        return t * inside(e)

    @pl.loop(0, E)
    def _(e):
        t = tort_of(e)
        tpad[e, pl.ds(8, Y), :] = t

    @pl.loop(0, E)
    def _(e):
        t = tpad[e, pl.ds(8, Y), :]
        right = 0.5 * (t + jnp.where(lane == X - 1, 0.0, pltpu.roll(t, X - 1, 1)))
        left = 0.5 * (t + jnp.where(lane == 0, 0.0, pltpu.roll(t, 1, 1)))
        north = 0.5 * (t + tpad[e, pl.ds(7, Y), :])
        south = 0.5 * (t + tpad[e, pl.ds(9, Y), :])
        total = right + left + north + south
        right = jnp.where(lane == X - 1, 0.0, right)
        left = jnp.where(lane == 0, 0.0, left)
        nxt = tpad[jnp.minimum(e + 1, E - 1), pl.ds(8, Y), :]
        zface = 0.5 * (t + nxt)
        v = velx[e]
        for y in range(Y):
            for ref, val in ((cxr, right), (cxl, left), (diag, total), (cz, zface), (vz, v)):
                ref[y, e] = jnp.broadcast_to(val[y : y + 1], (8, X))
            fy[y, e] = jnp.broadcast_to(north[y : y + 1], (8, X))
        fy[Y, e] = jnp.broadcast_to(south[Y - 1 : Y], (8, X))

    ups = [uptake[g, pl.ds(pl.multiple_of(me * SP, SP), SP), :] for g in range(M)]

    @pl.loop(0, E)
    def _(e):
        m = matx[e]
        for y in range(Y):
            row = jnp.broadcast_to(m[y : y + 1], (SP, X))
            r = ups[0]
            for g in range(1, M):
                r = jnp.where(row == g, ups[g], r)
            ratio[y, e] = r

    def react(st):
        @pl.loop(0, L // 2)
        def _(p):
            def both(a):
                return jnp.concatenate([a, a], axis=1)

            def band(l):
                return recv_a[st, :, l].reshape(S, X)

            l0 = 2 * p
            gathered = jnp.concatenate([band(l0), band(l0 + 1)], axis=1)
            inhibition = jnp.dot(inhibit_ref[...], gathered, preferred_element_type=f32)
            boost = jnp.dot(priming_ref[...], gathered, preferred_element_type=f32)
            dissolved = gathered.astype(f32)
            rate = both(mr[...]) * (1.0 + boost) / (both(hs[...]) + dissolved + inhibition)
            remaining = dissolved * jnp.exp(-rate)
            consumed = (dissolved - remaining).astype(bf16)
            roots = jnp.concatenate([root_b[pl.ds(l0, 1), :], root_b[pl.ds(l0 + 1, 1), :]], axis=1)
            reacted = (
                remaining
                + jnp.dot(produce_ref[...], consumed, preferred_element_type=f32)
                + both(ex[...]) * jnp.broadcast_to(roots, (S, 2 * X))
            )
            renewed = reacted.astype(bf16)
            low = (reacted - renewed.astype(f32)).astype(bf16)
            a16 = aff[...].astype(bf16)
            s_hi = jnp.dot(a16, renewed, preferred_element_type=f32)
            s_lo = jnp.dot(a16, low, preferred_element_type=f32)
            sums = s_hi[0:M] + s_hi[M:] + s_lo[0:M]
            for i in range(2):
                cols = slice(i * X, (i + 1) * X)
                labels = mat_ref[l0 + i, pl.ds(me, 1), :]
                hit = jnp.broadcast_to(labels, (M, X)) == lax.broadcasted_iota(jnp.int32, (M, X), 0)
                d = 1.0 + jnp.sum(jnp.where(hit, sums[:, cols], 0.0), axis=0, keepdims=True)
                den_send[st, p // 2, pl.ds(lax.rem(l0, SUB) + i, 1), :] = d
                send_b[st, :, l0 + i] = renewed[:, cols].reshape(N, SP, X)

    def prep(st, es, rim):
        @pl.loop(0, Y)
        def _(y):
            for e in es:
                r = ren[st, y, e].astype(f32)
                d = jnp.broadcast_to(den[st, y, e // SUB, e % SUB : e % SUB + 1, :], (SP, X))
                s = d / (d + ratio[y, e])
                if rim:
                    s = s * inside(e)
                fld[y, e] = r
                share[y, e] = s
                mob[0, y + 1, e] = s * r

    def substep(k, es, finish=None):
        last = k == SUB - 1

        @pl.loop(1, N + 1)
        def _(j):
            y = lax.rem(me + j, N)
            a = es[0]
            halves = (pl.ds(0, 8), pl.ds(8, 8))
            cen = [mob[k, y + 1, a, h, :] for h in halves]
            prev = [mob[k, y + 1, a - 1, h, :] for h in halves]
            czp, vp = cz[y, a - 1], vz[y, a - 1]
            fzp = [czp * (cen[i] - prev[i]) for i in range(2)]
            wp = [vp * prev[i] for i in range(2)]
            for e in es:
                cze, ve = cz[y, e], vz[y, e]
                xr, xl, n_, s_, dg = cxr[y, e], cxl[y, e], fy[y, e], fy[y + 1, e], diag[y, e]
                done = []
                for i, h in enumerate(halves):
                    m = cen[i]
                    nxt = mob[k, y + 1, e + 1, h, :]
                    fz = cze * (nxt - m)
                    w = ve * m
                    acc = fz - fzp[i]
                    acc += xr * pltpu.roll(m, X - 1, 1) + xl * pltpu.roll(m, 1, 1)
                    acc += n_ * mob[k, y, e, h, :] + s_ * mob[k, y + 2, e, h, :]
                    acc -= dg * m
                    f = fld[y, e, h, :] + (wp[i] - w) + dif_h[i] * acc
                    if last:
                        done.append(f)
                    else:
                        fld[y, e, h, :] = f
                        mob[k + 1, y + 1, e, h, :] = share[y, e, h, :] * f
                    cen[i], fzp[i], wp[i] = nxt, fz, w
                if last:
                    finish(y, e - SUB, jnp.concatenate(done, axis=0))
            if last:
                finish(y, None, j)

    for st in range(STEPS):
        recv_a[st, me] = send_a[st, me]

        @pl.loop(1, N)
        def _(d):
            wait_a(st, lax.rem(me + N - d, N))

        react(st)

        @pl.loop(1, N)
        def _(d):
            t = lax.rem(me + d, N)
            copy_d(st, t).start()
            copy_b(st, t).start()

        ren[st, me, pl.ds(SUB, L)] = send_b[st, me]
        den[st, me, pl.ds(1, 2)] = den_send[st]
        for cp in copies_h(st, me):
            cp.start()

        @pl.loop(1, N)
        def _(d):
            src = lax.rem(me + N - d, N)
            wait_d(st, src)
            wait_b(st, src)
            for cp in copies_h(st, src):
                cp.start()

        for cp in copies_g(st):
            cp.start()
        prep(st, range(SUB, SUB + L), False)
        for k in range(SUB - 1):
            substep(k, range(SUB + 1 + k, SUB + L - 1 - k))

        for cp in copies_g(st):
            cp.wait_recv()

        @pl.loop(0, Y)
        def _(y):
            for cp in copies_h(st, y):
                cp.wait_recv()

        prep(st, [*range(0, SUB), *range(SUB + L, E)], True)
        for k in range(SUB - 1):
            substep(k, range(k + 1, SUB + 1 + k))
            substep(k, range(SUB + L - 1 - k, E - 1 - k))
        if st < STEPS - 1:

            def finish(y, l, f):
                if l is not None:
                    send_a[st + 1, y, l] = f.astype(bf16)
                else:

                    @pl.when(f < N)
                    def _():
                        copy_a(st + 1, y, me).start()

        else:

            def finish(y, l, f):
                if l is not None:
                    outs[pl.ds(pl.multiple_of(l * Y * SP + y * SP, SP), SP), :] = f

        substep(SUB - 1, range(SUB, SUB + L), finish)

    @pl.loop(0, SP)
    def _(s):
        for l in range(L):
            out_ref[s, l] = outs[pl.ds(l * Y * SP + s, Y, stride=SP), :].astype(bf16)

    for cp in rims:
        cp.wait_send()
    for st in range(STEPS):

        @pl.loop(1, N)
        def _(d):
            t = lax.rem(me + d, N)
            wait_a_sent(st, t)
            copy_d(st, t).wait_send()
            copy_b(st, t).wait_send()

        @pl.loop(0, Y)
        def _(y):
            for cp in copies_h(st, y):
                cp.wait_send()

        for cp in copies_g(st):
            cp.wait_send()


def body(
    concentration, inhibit, priming, produce, max_rate, half_saturation, exudate,
    sorption_capacity, sorption_affinity, tortuosity, diffusivity, velocity, material, root_mask,
):
    vectors = jnp.stack([max_rate, half_saturation, exudate]).reshape(6, 128)
    vmem = pl.BlockSpec(memory_space=pltpu.VMEM)
    dma = pltpu.SemaphoreType.DMA
    big = (Y, E, SP, X)
    rep = (Y, E, 8, X)
    return pl.pallas_call(
        kernel,
        out_shape=jax.ShapeDtypeStruct((SP, L, Y, X), bf16),
        in_specs=[vmem] * 7 + [pl.BlockSpec(memory_space=pltpu.SMEM)] + [vmem] * 4,
        out_specs=vmem,
        scratch_shapes=[
            pltpu.VMEM((SP * L * Y, X), f32),
            pltpu.VMEM((STEPS, N, L, SP, X), bf16),
            pltpu.VMEM((STEPS, N, L, SP, X), bf16),
            pltpu.VMEM((STEPS, N, L, SP, X), bf16),
            pltpu.VMEM((STEPS, Y, E, SP, X), bf16),
            pltpu.VMEM((STEPS, 2, SUB, X), f32),
            pltpu.VMEM((STEPS, Y, 4, SUB, X), f32),
            pltpu.VMEM((E, Y, X), jnp.int32),
            pltpu.VMEM((E, Y, X), f32),
            pltpu.VMEM((E, 32, X), f32),
            pltpu.VMEM(rep, f32),
            pltpu.VMEM(rep, f32),
            pltpu.VMEM((Y + 1, E, 8, X), f32),
            pltpu.VMEM(rep, f32),
            pltpu.VMEM(rep, f32),
            pltpu.VMEM(rep, f32),
            pltpu.VMEM(big, f32),
            pltpu.VMEM((M, S, X), f32),
            pltpu.VMEM((S, X), f32),
            pltpu.VMEM((S, X), f32),
            pltpu.VMEM((S, X), f32),
            pltpu.VMEM((2 * M, S), f32),
            pltpu.VMEM((L, X), f32),
            pltpu.VMEM(big, f32),
            pltpu.VMEM(big, f32),
            pltpu.VMEM((SUB, Y + 2, E, SP, X), f32),
            pltpu.VMEM((L * Y * SP, X), f32),
            dma((STEPS, N)), dma((STEPS, N)),
            dma((STEPS, N)), dma((STEPS, N)),
            dma((STEPS, N)), dma((STEPS, N)),
            dma((STEPS, 2, Y)), dma((STEPS, 2, Y)),
            dma((STEPS, 2)), dma((STEPS, 2)),
            dma((4,)), dma((4,)),
        ],
        compiler_params=pltpu.CompilerParams(
            collective_id=0, has_side_effects=True, vmem_limit_bytes=48 * 2**20
        ),
    )(
        concentration, inhibit, priming, produce, vectors, sorption_capacity, sorption_affinity, tortuosity,
        diffusivity.reshape(1, SP), velocity, material, root_mask,
    )


def solution(mesh):
    in_specs = (
        P("spec", "slab", None, None),
        P(), P(), P(), P(), P(), P(), P(), P(), P(),
        P("spec"),
        P("slab", None, None),
        P("slab", None, None),
        P("slab", None, None),
    )
    out_specs = P("spec", "slab", None, None)
    return jax.shard_map(body, mesh=mesh, in_specs=in_specs, out_specs=out_specs, check_vma=False)
```

```python
import functools

import jax
import jax.numpy as jnp
from jax import lax
from jax.experimental import pallas as pl
from jax.experimental.pallas import tpu as pltpu
from jax.sharding import PartitionSpec as P

SUB = 4
STEPS = 2
N = 16
NSLAB = 16
SP = 16
L = 8
E = L + 2 * SUB
Y = 16
X = 128
S = 256
M = 8
MESH = pl.DeviceIdType.MESH
f32 = jnp.float32
bf16 = jnp.bfloat16


def column(row):
    n = row.shape[1]
    eye = lax.broadcasted_iota(jnp.int32, (n, n), 0) == lax.broadcasted_iota(jnp.int32, (n, n), 1)
    return jnp.sum(jnp.where(eye, jnp.broadcast_to(row, (n, n)), 0.0), axis=1, keepdims=True)


def kernel(
    c_hbm, inhibit_hbm, priming_hbm, produce_hbm, rate_hbm, half_hbm, exudate_hbm, capacity_hbm, affinity_hbm,
    tort_hbm, dif_hbm, vel_hbm, mat_hbm, root_hbm, out_ref,
    c_ref, inhibit_ref, priming_ref, produce_ref, rate_ref, half_ref, exudate_ref, capacity_ref, affinity_ref,
    tort_ref, dif_ref, root_ref, sem_in,
    c32, send_a, recv_a, send_b, ren, den_send, den,
    matx, velx, tpad, cxr, cxl, fy, diag, cz, vz, ratio, uptake, mr, hs, ex, aff, root_b,
    fld, share, mob0, mob1, mob2, mob3, outs,
    sem_as, sem_ar, sem_bs, sem_br, sem_ds, sem_dr, sem_hs, sem_hr, sem_gs, sem_gr, sem_cs, sem_cr,
):
    mob = (mob0, mob1, mob2, mob3)
    me = lax.axis_index("spec")
    slab = lax.axis_index("slab")
    below = lax.rem(slab + 1, NSLAB)
    above = lax.rem(slab + NSLAB - 1, NSLAB)

    own = pl.ds(SUB, L)
    loads = [
        pltpu.make_async_copy(src, dst, sem_in.at[i])
        for i, (src, dst) in enumerate((
            (c_hbm, c_ref), (mat_hbm, matx.at[own]), (vel_hbm, velx.at[own]), (tort_hbm, tort_ref),
            (capacity_hbm, capacity_ref), (affinity_hbm, affinity_ref), (rate_hbm, rate_ref), (half_hbm, half_ref),
            (exudate_hbm, exudate_ref), (dif_hbm, dif_ref), (root_hbm, root_ref), (inhibit_hbm, inhibit_ref),
            (priming_hbm, priming_ref), (produce_hbm, produce_ref),
        ))
    ]
    for cp in loads:
        cp.start()

    barrier = pltpu.get_barrier_semaphore()

    @pl.loop(1, N)
    def _(d):
        pl.semaphore_signal(barrier, inc=1, device_id={"spec": lax.rem(me + d, N)}, device_id_type=MESH)

    for t in (below, above):
        pl.semaphore_signal(barrier, inc=1, device_id={"slab": t}, device_id_type=MESH)

    loads[0].wait()

    @pl.loop(0, SP)
    def _(s):
        for l in range(L):
            c32[pl.ds(s * L * Y + l * Y, Y), :] = c_ref[s, l].astype(f32)

    pl.semaphore_wait(barrier, N + 1)

    def half(q):
        return pl.ds(q * SUB, SUB)

    def copy_a(st, q, t, slot):
        return pltpu.make_async_remote_copy(
            send_a.at[st, t, half(q)], recv_a.at[st, slot, half(q)], sem_as.at[st, q, t], sem_ar.at[st, q, slot],
            device_id={"spec": t}, device_id_type=MESH,
        )

    def copy_b(st, q, t, slot):
        return pltpu.make_async_remote_copy(
            send_b.at[st, t, half(q)], ren.at[st, slot, pl.ds(SUB + q * SUB, SUB)], sem_bs.at[st, q, t],
            sem_br.at[st, q, slot], device_id={"spec": t}, device_id_type=MESH,
        )

    def copy_d(st, q, t, slot):
        return pltpu.make_async_remote_copy(
            den_send.at[st, q], den.at[st, slot, 1 + q], sem_ds.at[st, q, t], sem_dr.at[st, q, slot],
            device_id={"spec": t}, device_id_type=MESH,
        )

    def copy_h(st, q, y):
        return pltpu.make_async_remote_copy(
            ren.at[st, y, pl.ds(SUB + q * SUB, SUB)], ren.at[st, y, pl.ds((1 - q) * (SUB + L), SUB)],
            sem_hs.at[st, q, y], sem_hr.at[st, q, y],
            device_id={"slab": below if q else above}, device_id_type=MESH,
        )

    def copy_g(st, q):
        return pltpu.make_async_remote_copy(
            den.at[st, :, 1 + q], den.at[st, :, 3 * (1 - q)], sem_gs.at[st, q], sem_gr.at[st, q],
            device_id={"slab": below if q else above}, device_id_type=MESH,
        )

    def copies_c():
        out = []
        for i, ref in enumerate((matx, velx)):
            out.append(pltpu.make_async_remote_copy(
                ref.at[pl.ds(L, SUB)], ref.at[pl.ds(0, SUB)], sem_cs.at[2 * i], sem_cr.at[2 * i],
                device_id={"slab": below}, device_id_type=MESH,
            ))
            out.append(pltpu.make_async_remote_copy(
                ref.at[pl.ds(SUB, SUB)], ref.at[pl.ds(L + SUB, SUB)], sem_cs.at[2 * i + 1], sem_cr.at[2 * i + 1],
                device_id={"slab": above}, device_id_type=MESH,
            ))
        return out

    for q in range(2):

        @pl.loop(1, N + 1)
        def _(d):
            t = lax.rem(me + d, N)
            for l in range(q * SUB, q * SUB + SUB):
                send_a[0, t, l] = c32[pl.ds(l * Y + t, SP, stride=L * Y), :].astype(bf16)

            @pl.when(d < N)
            def _():
                copy_a(0, q, t, me).start()

    for cp in loads[1:]:
        cp.wait()
    rims = copies_c()
    for cp in rims:
        cp.start()

    for i in range(2):
        rows = pl.ds(i * 128, 128)
        for ref, src in ((mr, rate_ref), (hs, half_ref), (ex, exudate_ref)):
            ref[rows, :] = jnp.broadcast_to(column(src[:, rows]), (128, X))
        for g in range(M):
            up = capacity_ref[g : g + 1, rows] * affinity_ref[g : g + 1, rows]
            uptake[g, rows, :] = jnp.broadcast_to(column(up), (128, X))
    a_hi = affinity_ref[...].astype(bf16)
    aff[0:M, :] = a_hi.astype(f32)
    aff[M : 2 * M, :] = affinity_ref[...] - a_hi.astype(f32)
    for l in range(L):
        root_b[l : l + 1, :] = root_ref[l, pl.ds(me, 1), :].astype(f32)
    dif = jnp.broadcast_to(column(dif_ref[...]), (SP, X))
    dif_h = (dif[0:8], dif[8:16])
    lane = lax.broadcasted_iota(jnp.int32, (Y, X), 1)
    zero_row = jnp.zeros((SP, X), f32)
    tpad[...] = jnp.zeros_like(tpad)
    for k in range(SUB):
        for e in range(E):
            mob[k][0, e] = zero_row
            mob[k][Y + 1, e] = zero_row

    for cp in rims:
        cp.wait_recv()

    def inside(e):
        layer = slab * L + e - SUB
        return jnp.where((layer >= 0) & (layer < NSLAB * L), 1.0, 0.0).astype(f32)

    torts = [jnp.broadcast_to(tort_ref[:, g : g + 1], (Y, X)) for g in range(M)]

    def tort_of(e):
        m = matx[e]
        t = jnp.zeros((Y, X), f32)
        for g in range(M):
            t = jnp.where(m == g, torts[g], t)
        return t * inside(e)

    @pl.loop(0, E)
    def _(e):
        t = tort_of(e)
        tpad[e, pl.ds(8, Y), :] = t

    @pl.loop(0, E)
    def _(e):
        t = tpad[e, pl.ds(8, Y), :]
        right = 0.5 * (t + jnp.where(lane == X - 1, 0.0, pltpu.roll(t, X - 1, 1)))
        left = 0.5 * (t + jnp.where(lane == 0, 0.0, pltpu.roll(t, 1, 1)))
        north = 0.5 * (t + tpad[e, pl.ds(7, Y), :])
        south = 0.5 * (t + tpad[e, pl.ds(9, Y), :])
        total = right + left + north + south
        right = jnp.where(lane == X - 1, 0.0, right)
        left = jnp.where(lane == 0, 0.0, left)
        nxt = tpad[jnp.minimum(e + 1, E - 1), pl.ds(8, Y), :]
        zface = 0.5 * (t + nxt)
        v = velx[e]
        for y in range(Y):
            for ref, val in ((cxr, right), (cxl, left), (diag, total), (cz, zface), (vz, v)):
                ref[y, e] = jnp.broadcast_to(val[y : y + 1], (8, X))
            fy[y, e] = jnp.broadcast_to(north[y : y + 1], (8, X))
        fy[Y, e] = jnp.broadcast_to(south[Y - 1 : Y], (8, X))

    ups = [uptake[g, pl.ds(pl.multiple_of(me * SP, SP), SP), :] for g in range(M)]

    @pl.loop(0, E)
    def _(e):
        m = matx[e]
        for y in range(Y):
            row = jnp.broadcast_to(m[y : y + 1], (SP, X))
            r = ups[0]
            for g in range(1, M):
                r = jnp.where(row == g, ups[g], r)
            ratio[y, e] = r

    def react(st, q):
        @pl.loop(q * SUB // 2, (q + 1) * SUB // 2)
        def _(p):
            def both(a):
                return jnp.concatenate([a, a], axis=1)

            def band(l):
                return recv_a[st, :, l].reshape(S, X)

            l0 = 2 * p
            gathered = jnp.concatenate([band(l0), band(l0 + 1)], axis=1)
            inhibition = jnp.dot(inhibit_ref[...], gathered, preferred_element_type=f32)
            boost = jnp.dot(priming_ref[...], gathered, preferred_element_type=f32)
            dissolved = gathered.astype(f32)
            rate = both(mr[...]) * (1.0 + boost) / (both(hs[...]) + dissolved + inhibition)
            remaining = dissolved * jnp.exp(-rate)
            consumed = (dissolved - remaining).astype(bf16)
            roots = jnp.concatenate([root_b[pl.ds(l0, 1), :], root_b[pl.ds(l0 + 1, 1), :]], axis=1)
            reacted = (
                remaining
                + jnp.dot(produce_ref[...], consumed, preferred_element_type=f32)
                + both(ex[...]) * jnp.broadcast_to(roots, (S, 2 * X))
            )
            renewed = reacted.astype(bf16)
            low = (reacted - renewed.astype(f32)).astype(bf16)
            a16 = aff[...].astype(bf16)
            s_hi = jnp.dot(a16, renewed, preferred_element_type=f32)
            s_lo = jnp.dot(a16, low, preferred_element_type=f32)
            sums = s_hi[0:M] + s_hi[M:] + s_lo[0:M]
            for i in range(2):
                cols = slice(i * X, (i + 1) * X)
                labels = matx[SUB + l0 + i, pl.ds(me, 1), :]
                hit = jnp.broadcast_to(labels, (M, X)) == lax.broadcasted_iota(jnp.int32, (M, X), 0)
                d = 1.0 + jnp.sum(jnp.where(hit, sums[:, cols], 0.0), axis=0, keepdims=True)
                den_send[st, q, pl.ds(l0 - q * SUB + i, 1), :] = d
                send_b[st, :, l0 + i] = renewed[:, cols].reshape(N, SP, X)

    def prep(st, es, rim):
        @pl.loop(0, Y)
        def _(y):
            vals = []
            for e in es:
                r = ren[st, y, e].astype(f32)
                d = jnp.broadcast_to(den[st, y, e // SUB, e % SUB : e % SUB + 1, :], (SP, X))
                s = d / (d + ratio[y, e])
                if rim:
                    s = s * inside(e)
                vals.append((r, s))
            for e, (r, s) in zip(es, vals):
                fld[y, e] = r
                share[y, e] = s
                mob[0][y + 1, e] = s * r

    def substep(k, spans, rows, finish=None):
        last = k == SUB - 1
        halves = (pl.ds(0, 8), pl.ds(8, 8))

        def span(y, es):
            a = es[0]
            cen = [mob[k][y + 1, a, h, :] for h in halves]
            prev = [mob[k][y + 1, a - 1, h, :] for h in halves]
            czp, vp = cz[y, a - 1], vz[y, a - 1]
            fzp = [czp * (cen[i] - prev[i]) for i in range(2)]
            wp = [vp * prev[i] for i in range(2)]
            done = []
            for e in es:
                cze, ve = cz[y, e], vz[y, e]
                xr, xl, n_, s_, dg = cxr[y, e], cxl[y, e], fy[y, e], fy[y + 1, e], diag[y, e]
                for i, h in enumerate(halves):
                    m = cen[i]
                    nxt = mob[k][y + 1, e + 1, h, :]
                    fz = cze * (nxt - m)
                    w = ve * m
                    acc = fz - fzp[i]
                    acc += xr * pltpu.roll(m, X - 1, 1) + xl * pltpu.roll(m, 1, 1)
                    acc += n_ * mob[k][y, e, h, :] + s_ * mob[k][y + 2, e, h, :]
                    acc -= dg * m
                    done.append(fld[y, e, h, :] + (wp[i] - w) + dif_h[i] * acc)
                    cen[i], fzp[i], wp[i] = nxt, fz, w
            if last:
                for i, e in enumerate(es):
                    finish(y, e - SUB, jnp.concatenate(done[2 * i : 2 * i + 2], axis=0))
            else:
                out = [share[y, e, h, :] for e in es for h in halves]
                out = [a * b for a, b in zip(out, done)]
                for i, e in enumerate(es):
                    for n, h in enumerate(halves):
                        fld[y, e, h, :] = done[2 * i + n]
                        mob[k + 1][y + 1, e, h, :] = out[2 * i + n]

        @pl.loop(0, Y // rows)
        def _(j):
            ys = [lax.rem(me + j * rows + 1 + i, N) for i in range(rows)]
            for y in ys:
                for es in spans:
                    span(y, es)
            if last:
                for i, y in enumerate(ys):
                    finish(y, None, j * rows + 1 + i)

    for st in range(STEPS):
        recv_a[st, me] = send_a[st, me]
        for q in range(2):

            @pl.loop(1, N)
            def _(d):
                src = lax.rem(me + N - d, N)
                copy_a(st, q, src, src).wait_recv()

            react(st, q)

            @pl.loop(1, N)
            def _(d):
                t = lax.rem(me + d, N)
                copy_d(st, q, t, me).start()
                copy_b(st, q, t, me).start()

            ren[st, me, pl.ds(SUB + q * SUB, SUB)] = send_b[st, me, half(q)]
            den[st, me, 1 + q] = den_send[st, q]
            copy_h(st, q, me).start()

        for q in range(2):

            @pl.loop(1, N)
            def _(d):
                src = lax.rem(me + N - d, N)
                copy_d(st, q, src, src).wait_recv()
                copy_b(st, q, src, src).wait_recv()
                copy_h(st, q, src).start()

            copy_g(st, q).start()

        prep(st, range(SUB, SUB + L), False)
        for k in range(SUB - 1):
            substep(k, [range(SUB + 1 + k, SUB + L - 1 - k)], (4, 8, 16)[k])

        for q in range(2):
            copy_g(st, q).wait_recv()

            @pl.loop(0, Y)
            def _(y):
                copy_h(st, q, y).wait_recv()

        prep(st, [*range(0, SUB), *range(SUB + L, E)], True)
        for k in range(SUB - 1):
            substep(k, [range(k + 1, SUB + 1 + k), range(SUB + L - 1 - k, E - 1 - k)], 4)
        for q in range(2):
            if st < STEPS - 1:

                def finish(y, l, f):
                    if l is not None:
                        send_a[st + 1, y, l] = f.astype(bf16)
                    else:

                        @pl.when(f < N)
                        def _():
                            copy_a(st + 1, q, y, me).start()

            else:

                def finish(y, l, f):
                    if l is not None:
                        outs[pl.ds(pl.multiple_of(l * Y * SP + y * SP, SP), SP), :] = f

            substep(SUB - 1, [range(SUB + q * SUB, SUB + (q + 1) * SUB)], 8, finish)

    @pl.loop(0, SP)
    def _(s):
        for l in range(L):
            out_ref[s, l] = outs[pl.ds(l * Y * SP + s, Y, stride=SP), :].astype(bf16)

    for cp in rims:
        cp.wait_send()
    for st in range(STEPS):
        for q in range(2):

            @pl.loop(1, N)
            def _(d):
                t = lax.rem(me + d, N)
                copy_a(st, q, t, me).wait_send()
                copy_d(st, q, t, me).wait_send()
                copy_b(st, q, t, me).wait_send()

            @pl.loop(0, Y)
            def _(y):
                copy_h(st, q, y).wait_send()

            copy_g(st, q).wait_send()


def body(
    concentration, inhibit, priming, produce, max_rate, half_saturation, exudate,
    sorption_capacity, sorption_affinity, tortuosity, diffusivity, velocity, material, root_mask,
):
    vmem = pl.BlockSpec(memory_space=pltpu.VMEM)
    dma = pltpu.SemaphoreType.DMA
    big = (Y, E, SP, X)
    rep = (Y, E, 8, X)
    return pl.pallas_call(
        kernel,
        out_shape=jax.ShapeDtypeStruct((SP, L, Y, X), bf16),
        in_specs=[pl.BlockSpec(memory_space=pltpu.HBM)] * 14,
        out_specs=vmem,
        scratch_shapes=[
            pltpu.VMEM((SP, L, Y, X), bf16),
            pltpu.VMEM((S, S), bf16), pltpu.VMEM((S, S), bf16), pltpu.VMEM((S, S), bf16),
            pltpu.VMEM((1, S), f32), pltpu.VMEM((1, S), f32), pltpu.VMEM((1, S), f32),
            pltpu.VMEM((M, S), f32), pltpu.VMEM((M, S), f32),
            pltpu.VMEM((1, M), f32), pltpu.VMEM((1, SP), f32),
            pltpu.VMEM((L, Y, X), jnp.int32),
            dma((14,)),
            pltpu.VMEM((SP * L * Y, X), f32),
            pltpu.VMEM((STEPS, N, L, SP, X), bf16),
            pltpu.VMEM((STEPS, N, L, SP, X), bf16),
            pltpu.VMEM((STEPS, N, L, SP, X), bf16),
            pltpu.VMEM((STEPS, Y, E, SP, X), bf16),
            pltpu.VMEM((STEPS, 2, SUB, X), f32),
            pltpu.VMEM((STEPS, Y, 4, SUB, X), f32),
            pltpu.VMEM((E, Y, X), jnp.int32),
            pltpu.VMEM((E, Y, X), f32),
            pltpu.VMEM((E, 32, X), f32),
            pltpu.VMEM(rep, f32),
            pltpu.VMEM(rep, f32),
            pltpu.VMEM((Y + 1, E, 8, X), f32),
            pltpu.VMEM(rep, f32),
            pltpu.VMEM(rep, f32),
            pltpu.VMEM(rep, f32),
            pltpu.VMEM(big, f32),
            pltpu.VMEM((M, S, X), f32),
            pltpu.VMEM((S, X), f32),
            pltpu.VMEM((S, X), f32),
            pltpu.VMEM((S, X), f32),
            pltpu.VMEM((2 * M, S), f32),
            pltpu.VMEM((L, X), f32),
            pltpu.VMEM(big, f32),
            pltpu.VMEM(big, f32),
            *[pltpu.VMEM((Y + 2, E, SP, X), f32)] * SUB,
            pltpu.VMEM((L * Y * SP, X), f32),
            dma((STEPS, 2, N)), dma((STEPS, 2, N)),
            dma((STEPS, 2, N)), dma((STEPS, 2, N)),
            dma((STEPS, 2, N)), dma((STEPS, 2, N)),
            dma((STEPS, 2, Y)), dma((STEPS, 2, Y)),
            dma((STEPS, 2)), dma((STEPS, 2)),
            dma((4,)), dma((4,)),
        ],
        compiler_params=pltpu.CompilerParams(
            collective_id=0, has_side_effects=True, vmem_limit_bytes=64 * 2**20 - 65536
        ),
    )(
        concentration, inhibit, priming, produce, max_rate.reshape(1, S), half_saturation.reshape(1, S),
        exudate.reshape(1, S), sorption_capacity, sorption_affinity, tortuosity.reshape(1, M),
        diffusivity.reshape(1, SP), velocity, material, root_mask,
    )


def solution(mesh):
    in_specs = (
        P("spec", "slab", None, None),
        P(), P(), P(), P(), P(), P(), P(), P(), P(),
        P("spec"),
        P("slab", None, None),
        P("slab", None, None),
        P("slab", None, None),
    )
    out_specs = P("spec", "slab", None, None)
    return jax.shard_map(body, mesh=mesh, in_specs=in_specs, out_specs=out_specs, check_vma=False)
```

```python
import functools

import jax
import jax.numpy as jnp
from jax import lax
from jax.experimental import pallas as pl
from jax.experimental.pallas import tpu as pltpu
from jax.sharding import PartitionSpec as P

SUB = 4
STEPS = 2
N = 16
NSLAB = 16
SP = 16
L = 8
E = L + 2 * SUB
Y = 16
X = 128
S = 256
M = 8
MESH = pl.DeviceIdType.MESH
f32 = jnp.float32
bf16 = jnp.bfloat16


def column(row):
    n = row.shape[1]
    eye = lax.broadcasted_iota(jnp.int32, (n, n), 0) == lax.broadcasted_iota(jnp.int32, (n, n), 1)
    return jnp.sum(jnp.where(eye, jnp.broadcast_to(row, (n, n)), 0.0), axis=1, keepdims=True)


def kernel(
    c_hbm, inhibit_hbm, priming_hbm, produce_hbm, rate_hbm, half_hbm, exudate_hbm, capacity_hbm, affinity_hbm,
    tort_hbm, dif_hbm, vel_hbm, mat_hbm, root_hbm, out_ref,
    c_ref, inhibit_ref, priming_ref, produce_ref, rate_ref, half_ref, exudate_ref, capacity_ref, affinity_ref,
    tort_ref, dif_ref, root_ref, sem_in,
    c32, send_a, recv_a, send_b, ren, den_send, den,
    matx, velx, tpad, cxr, cxl, fy, diag, cz, vz, ratio, uptake, mr, hs, ex, aff, root_b,
    fld, share, mob0, mob1, mob2, mob3, outs,
    sem_as, sem_ar, sem_bs, sem_br, sem_ds, sem_dr, sem_hs, sem_hr, sem_gs, sem_gr, sem_cs, sem_cr,
):
    mob = (mob0, mob1, mob2, mob3)
    me = lax.axis_index("spec")
    slab = lax.axis_index("slab")
    below = lax.rem(slab + 1, NSLAB)
    above = lax.rem(slab + NSLAB - 1, NSLAB)

    own = pl.ds(SUB, L)
    loads = [
        pltpu.make_async_copy(src, dst, sem_in.at[i])
        for i, (src, dst) in enumerate((
            (c_hbm, c_ref), (mat_hbm, matx.at[own]), (vel_hbm, velx.at[own]), (tort_hbm, tort_ref),
            (capacity_hbm, capacity_ref), (affinity_hbm, affinity_ref), (rate_hbm, rate_ref), (half_hbm, half_ref),
            (exudate_hbm, exudate_ref), (dif_hbm, dif_ref), (root_hbm, root_ref), (inhibit_hbm, inhibit_ref),
            (priming_hbm, priming_ref), (produce_hbm, produce_ref),
        ))
    ]
    for cp in loads:
        cp.start()

    x, z = me // 4, lax.rem(me, 4)

    def at(dx, dz):
        return lax.rem(x + dx, 4) * 4 + lax.rem(z + dz, 4)

    far = (2, 1, 3, 0)
    partners = [at(dx, dz) for dx in far for dz in far if dx or dz]

    barrier = pltpu.get_barrier_semaphore()

    @pl.loop(1, N)
    def _(d):
        pl.semaphore_signal(barrier, inc=1, device_id={"spec": lax.rem(me + d, N)}, device_id_type=MESH)

    for t in (below, above):
        pl.semaphore_signal(barrier, inc=1, device_id={"slab": t}, device_id_type=MESH)

    loads[0].wait()

    @pl.loop(0, SP)
    def _(s):
        for l in range(L):
            c32[pl.ds(s * L * Y + l * Y, Y), :] = c_ref[s, l].astype(f32)

    @pl.loop(0, N)
    def _(t):
        for p in range(L // 2):
            v = [c32[pl.ds(l * Y + t, SP, stride=L * Y), :] for l in (2 * p, 2 * p + 1)]
            for h in range(2):
                pair = jnp.concatenate([v[0][8 * h : 8 * h + 8], v[1][8 * h : 8 * h + 8]], axis=0)
                send_a[0, t, h, p] = pair.astype(bf16)

    pl.semaphore_wait(barrier, N + 1)

    both = pl.ds(0, 2)
    parts_a = (((both, pl.ds(0, 2)), (both, pl.ds(2, 2))), ((pl.ds(0, 1), pl.ds(0, 4)), (pl.ds(1, 1), pl.ds(0, 2)), (pl.ds(1, 1), pl.ds(2, 2))))
    parts_b = ((both, 0), (pl.ds(0, 1), 1), (pl.ds(1, 1), 1))

    def copy_a(st, i, t, slot):
        hs, ps = parts_a[st][i]
        return pltpu.make_async_remote_copy(
            send_a.at[st, t, hs, ps], recv_a.at[st, slot, hs, ps], sem_as.at[st, i, t], sem_ar.at[st, i, slot],
            device_id={"spec": t}, device_id_type=MESH,
        )

    def copy_b(st, i, t, slot):
        hs, q = parts_b[i]
        return pltpu.make_async_remote_copy(
            send_b.at[st, t, hs, pl.ds(2 * q, 2)], ren.at[st, slot, hs, pl.ds(2 + 2 * q, 2)], sem_bs.at[st, i, t],
            sem_br.at[st, i, slot], device_id={"spec": t}, device_id_type=MESH,
        )

    def copy_d(st, q, slot, t, key):
        return pltpu.make_async_remote_copy(
            den.at[st, slot, 1 + q], den.at[st, slot, 1 + q], sem_ds.at[st, q, key], sem_dr.at[st, q, slot],
            device_id={"spec": t}, device_id_type=MESH,
        )

    def start_d(st, q, dz):
        for dx in (2, 1, 3):
            copy_d(st, q, at(0, dz), at(dx, 0), at(dx, dz)).start()

    def forward_d(st, q):
        for dz in (1, 3, 2):
            slot = at(0, dz)
            copy_d(st, q, slot, slot, slot).wait_recv()
            start_d(st, q, dz)

    def copy_h(st, i, y):
        hs, q = parts_b[i]
        return pltpu.make_async_remote_copy(
            ren.at[st, y, hs, pl.ds(2 + 2 * q, 2)], ren.at[st, y, hs, pl.ds(6 - 6 * q, 2)],
            sem_hs.at[st, i, y], sem_hr.at[st, i, y],
            device_id={"slab": below if q else above}, device_id_type=MESH,
        )

    def copy_g(st, q):
        return pltpu.make_async_remote_copy(
            den.at[st, :, 1 + q], den.at[st, :, 3 * (1 - q)], sem_gs.at[st, q], sem_gr.at[st, q],
            device_id={"slab": below if q else above}, device_id_type=MESH,
        )

    def copies_c():
        out = []
        for i, ref in enumerate((matx, velx)):
            out.append(pltpu.make_async_remote_copy(
                ref.at[pl.ds(L, SUB)], ref.at[pl.ds(0, SUB)], sem_cs.at[2 * i], sem_cr.at[2 * i],
                device_id={"slab": below}, device_id_type=MESH,
            ))
            out.append(pltpu.make_async_remote_copy(
                ref.at[pl.ds(SUB, SUB)], ref.at[pl.ds(L + SUB, SUB)], sem_cs.at[2 * i + 1], sem_cr.at[2 * i + 1],
                device_id={"slab": above}, device_id_type=MESH,
            ))
        return out

    def start_a(st, i):
        for t in partners:
            copy_a(st, i, t, me).start()

    start_a(0, 0)
    start_a(0, 1)

    for cp in loads[1:]:
        cp.wait()
    rims = copies_c()
    for cp in rims:
        cp.start()

    for i in range(2):
        rows = pl.ds(i * 128, 128)
        for ref, src in ((mr, rate_ref), (hs, half_ref), (ex, exudate_ref)):
            ref[rows, :] = jnp.broadcast_to(column(src[:, rows]), (128, X))
        for g in range(M):
            up = capacity_ref[g : g + 1, rows] * affinity_ref[g : g + 1, rows]
            uptake[g, rows, :] = jnp.broadcast_to(column(up), (128, X))
    a_hi = affinity_ref[...].astype(bf16)
    aff[0:M, :] = a_hi.astype(f32)
    aff[M : 2 * M, :] = affinity_ref[...] - a_hi.astype(f32)
    for l in range(L):
        root_b[l : l + 1, :] = root_ref[l, pl.ds(me, 1), :].astype(f32)
    dif = jnp.broadcast_to(column(dif_ref[...]), (SP, X))
    dif_h = (dif[0:8], dif[8:16])
    lane = lax.broadcasted_iota(jnp.int32, (Y, X), 1)
    zero_row = jnp.zeros((SP, X), f32)
    tpad[...] = jnp.zeros_like(tpad)
    for k in range(SUB):
        for e in range(E):
            mob[k][0, e] = zero_row
            mob[k][Y + 1, e] = zero_row

    for cp in rims:
        cp.wait_recv()

    def inside(e):
        layer = slab * L + e - SUB
        return jnp.where((layer >= 0) & (layer < NSLAB * L), 1.0, 0.0).astype(f32)

    torts = [jnp.broadcast_to(tort_ref[:, g : g + 1], (Y, X)) for g in range(M)]

    def tort_of(e):
        m = matx[e]
        t = jnp.zeros((Y, X), f32)
        for g in range(M):
            t = jnp.where(m == g, torts[g], t)
        return t * inside(e)

    @pl.loop(0, E)
    def _(e):
        t = tort_of(e)
        tpad[e, pl.ds(8, Y), :] = t

    @pl.loop(0, E)
    def _(e):
        t = tpad[e, pl.ds(8, Y), :]
        right = 0.5 * (t + jnp.where(lane == X - 1, 0.0, pltpu.roll(t, X - 1, 1)))
        left = 0.5 * (t + jnp.where(lane == 0, 0.0, pltpu.roll(t, 1, 1)))
        north = 0.5 * (t + tpad[e, pl.ds(7, Y), :])
        south = 0.5 * (t + tpad[e, pl.ds(9, Y), :])
        total = right + left + north + south
        right = jnp.where(lane == X - 1, 0.0, right)
        left = jnp.where(lane == 0, 0.0, left)
        nxt = tpad[jnp.minimum(e + 1, E - 1), pl.ds(8, Y), :]
        zface = 0.5 * (t + nxt)
        v = velx[e]
        for y in range(Y):
            for ref, val in ((cxr, right), (cxl, left), (diag, total), (cz, zface), (vz, v)):
                ref[y, e] = jnp.broadcast_to(val[y : y + 1], (8, X))
            fy[y, e] = jnp.broadcast_to(north[y : y + 1], (8, X))
        fy[Y, e] = jnp.broadcast_to(south[Y - 1 : Y], (8, X))

    ups = [uptake[g, pl.ds(pl.multiple_of(me * SP, SP), SP), :] for g in range(M)]

    @pl.loop(0, E)
    def _(e):
        m = matx[e]
        for y in range(Y):
            row = jnp.broadcast_to(m[y : y + 1], (SP, X))
            r = ups[0]
            for g in range(1, M):
                r = jnp.where(row == g, ups[g], r)
            ratio[y, e] = r

    def react(st, q):
        @pl.loop(q * SUB // 2, (q + 1) * SUB // 2)
        def _(p):
            def twice(a):
                return jnp.concatenate([a, a], axis=1)

            l0 = 2 * p
            pairs = recv_a[st, :, :, p].astype(f32).reshape(N, 2, 2, 8, X)
            dissolved = jnp.concatenate([pairs[:, :, i].reshape(S, X) for i in range(2)], axis=1)
            gathered = dissolved.astype(bf16)
            inhibition = jnp.dot(inhibit_ref[...], gathered, preferred_element_type=f32)
            boost = jnp.dot(priming_ref[...], gathered, preferred_element_type=f32)
            rate = twice(mr[...]) * (1.0 + boost) / (twice(hs[...]) + dissolved + inhibition)
            remaining = dissolved * jnp.exp(-rate)
            consumed = (dissolved - remaining).astype(bf16)
            roots = jnp.concatenate([root_b[pl.ds(l0, 1), :], root_b[pl.ds(l0 + 1, 1), :]], axis=1)
            reacted = (
                remaining
                + jnp.dot(produce_ref[...], consumed, preferred_element_type=f32)
                + twice(ex[...]) * jnp.broadcast_to(roots, (S, 2 * X))
            )
            renewed = reacted.astype(bf16)
            low = (reacted - renewed.astype(f32)).astype(bf16)
            a16 = aff[...].astype(bf16)
            s_hi = jnp.dot(a16, renewed, preferred_element_type=f32)
            s_lo = jnp.dot(a16, low, preferred_element_type=f32)
            sums = s_hi[0:M] + s_hi[M:] + s_lo[0:M]
            for i in range(2):
                cols = slice(i * X, (i + 1) * X)
                labels = matx[SUB + l0 + i, pl.ds(me, 1), :]
                hit = jnp.broadcast_to(labels, (M, X)) == lax.broadcasted_iota(jnp.int32, (M, X), 0)
                d = 1.0 + jnp.sum(jnp.where(hit, sums[:, cols], 0.0), axis=0, keepdims=True)
                den_send[st, q, pl.ds(l0 - q * SUB + i, 1), :] = d
            split = [reacted[:, i * X : (i + 1) * X].reshape(N, 2, 1, 8, X) for i in range(2)]
            send_b[st, :, :, p] = jnp.concatenate(split, axis=2).reshape(N, 2, SP, X).astype(bf16)

    def prep(st, h, pairs, rim):
        rows = pl.ds(8 * h, 8)

        @pl.loop(0, Y // 2)
        def _(j):
            vals = []
            for y in (2 * j, 2 * j + 1):
                for pair in pairs:
                    r2 = ren[st, y, h, pair].astype(f32)
                    for i in range(2):
                        e = 2 * pair + i
                        r = r2[8 * i : 8 * i + 8]
                        d = jnp.broadcast_to(den[st, y, e // SUB, e % SUB : e % SUB + 1, :], (8, X))
                        s = d / (d + ratio[y, e, rows, :])
                        if rim:
                            s = s * inside(e)
                        vals.append((y, e, r, s))
            for y, e, r, s in vals:
                fld[y, e, rows, :] = r
                share[y, e, rows, :] = s
                mob[0][y + 1, e, rows, :] = s * r

    def substep(k, h, spans, n, finish=None):
        hr = pl.ds(8 * h, 8)
        src = mob[k]

        @pl.loop(0, Y // n)
        def _(j):
            y0 = j * n
            for es in spans:
                a = es[0]
                cen = [src[y0 + 1 + i, a, hr, :] for i in range(n)]
                prev = [src[y0 + 1 + i, a - 1, hr, :] for i in range(n)]
                fzp = [cz[y0 + i, a - 1] * (cen[i] - prev[i]) for i in range(n)]
                wp = [vz[y0 + i, a - 1] * prev[i] for i in range(n)]
                before = None
                for e in es:
                    rows = [src[y0, e, hr, :]] + cen + [src[y0 + n + 1, e, hr, :]]
                    fyv = [fy[y0 + i, e] for i in range(n + 1)]
                    nxt = [src[y0 + 1 + i, e + 1, hr, :] for i in range(n)]
                    done = []
                    for i in range(n):
                        y, m = y0 + i, cen[i]
                        fz = cz[y, e] * (nxt[i] - m)
                        w = vz[y, e] * m
                        acc = fz - fzp[i]
                        acc += cxr[y, e] * pltpu.roll(m, X - 1, 1) + cxl[y, e] * pltpu.roll(m, 1, 1)
                        acc += fyv[i] * rows[i] + fyv[i + 1] * rows[i + 2]
                        acc -= diag[y, e] * m
                        f = fld[y, e, hr, :] + (wp[i] - w) + dif_h[h] * acc
                        fzp[i], wp[i] = fz, w
                        if finish is None:
                            fld[y, e, hr, :] = f
                            mob[k + 1][y + 1, e, hr, :] = share[y, e, hr, :] * f
                        else:
                            done.append(f)
                    cen = nxt
                    if finish is not None:
                        if e % 2:
                            for i in range(n):
                                finish(y0 + i, e - 1 - SUB, before[i], done[i])
                        before = done

    def own_part(st, h):
        prep(st, h, range(2, 6), False)
        for k in range(SUB - 1):
            substep(k, h, [range(SUB + 1 + k, SUB + L - 1 - k)], (8, 16, 16)[k])

    def rest(st, h):
        prep(st, h, (0, 1, 6, 7), True)
        for k in range(SUB - 1):
            substep(k, h, [range(k + 1, SUB + 1 + k), range(SUB + L - 1 - k, E - 1 - k)], 8)

        def finish(y, l, f0, f1):
            if st < STEPS - 1:
                send_a[st + 1, y, h, l // 2] = jnp.concatenate([f0, f1], axis=0).astype(bf16)
            else:
                for i, f in enumerate((f0, f1)):
                    outs[pl.ds(pl.multiple_of((l + i) * Y * SP + y * SP + 8 * h, 8), 8), :] = f

        for q in range(2):
            substep(SUB - 1, h, [range(SUB + q * SUB, SUB + (q + 1) * SUB)], 8, finish)
            if st < STEPS - 1 and (h or q):
                start_a(st + 1, h * (1 + q))

    for st in range(STEPS):
        recv_a[st, me] = send_a[st, me]
        for q in range(2):

            @pl.loop(1, N)
            def _(d):
                src = lax.rem(me + N - d, N)
                if st and q == 0:
                    copy_a(st, 0, src, src).wait_recv()
                copy_a(st, q + st, src, src).wait_recv()

            react(st, q)

            den[st, me, 1 + q] = den_send[st, q]
            if q:
                forward_d(st, 0)
            for dz in (2, 1, 3):
                t = at(0, dz)
                copy_d(st, q, me, t, t).start()
            start_d(st, q, 0)
            for t in partners:
                copy_b(st, q, t, me).start()
            ren[st, me, :, pl.ds(2 + 2 * q, 2)] = send_b[st, me, :, pl.ds(2 * q, 2)]
            copy_h(st, q, me).start()

        for t in partners:
            copy_b(st, 2, t, me).start()
        copy_h(st, 2, me).start()
        for q in range(2):

            @pl.loop(1, N)
            def _(d):
                src = lax.rem(me + N - d, N)
                copy_b(st, q, src, src).wait_recv()
                copy_h(st, q, src).start()

            if q == 0:
                forward_d(st, 1)

        for q in range(2):

            @pl.loop(4, N)
            def _(d):
                slot = lax.rem(x + d // 4, 4) * 4 + lax.rem(d, 4)
                copy_d(st, q, slot, slot, slot).wait_recv()

            copy_g(st, q).start()

        own_part(st, 0)

        @pl.loop(1, N)
        def _(d):
            src = lax.rem(me + N - d, N)
            copy_b(st, 2, src, src).wait_recv()
            copy_h(st, 2, src).start()

        for q in range(2):
            copy_g(st, q).wait_recv()

            @pl.loop(0, Y)
            def _(y):
                copy_h(st, q, y).wait_recv()

        rest(st, 0)
        own_part(st, 1)

        @pl.loop(0, Y)
        def _(y):
            copy_h(st, 2, y).wait_recv()

        rest(st, 1)

    @pl.loop(0, SP)
    def _(s):
        for l in range(L):
            out_ref[s, l] = outs[pl.ds(l * Y * SP + s, Y, stride=SP), :].astype(bf16)

    for cp in rims:
        cp.wait_send()
    for st in range(STEPS):

        @pl.loop(1, N)
        def _(d):
            t = lax.rem(me + d, N)
            for i in range(len(parts_a[st])):
                copy_a(st, i, t, me).wait_send()
            for i in range(3):
                copy_b(st, i, t, me).wait_send()
            for q in range(2):
                copy_d(st, q, t, t, t).wait_send()

        @pl.loop(0, Y)
        def _(y):
            for i in range(3):
                copy_h(st, i, y).wait_send()

        for q in range(2):
            copy_g(st, q).wait_send()


def body(
    concentration, inhibit, priming, produce, max_rate, half_saturation, exudate,
    sorption_capacity, sorption_affinity, tortuosity, diffusivity, velocity, material, root_mask,
):
    vmem = pl.BlockSpec(memory_space=pltpu.VMEM)
    dma = pltpu.SemaphoreType.DMA
    big = (Y, E, SP, X)
    rep = (Y, E, 8, X)
    return pl.pallas_call(
        kernel,
        out_shape=jax.ShapeDtypeStruct((SP, L, Y, X), bf16),
        in_specs=[pl.BlockSpec(memory_space=pltpu.HBM)] * 14,
        out_specs=vmem,
        scratch_shapes=[
            pltpu.VMEM((SP, L, Y, X), bf16),
            pltpu.VMEM((S, S), bf16), pltpu.VMEM((S, S), bf16), pltpu.VMEM((S, S), bf16),
            pltpu.VMEM((1, S), f32), pltpu.VMEM((1, S), f32), pltpu.VMEM((1, S), f32),
            pltpu.VMEM((M, S), f32), pltpu.VMEM((M, S), f32),
            pltpu.VMEM((1, M), f32), pltpu.VMEM((1, SP), f32),
            pltpu.VMEM((L, Y, X), jnp.int32),
            dma((14,)),
            pltpu.VMEM((SP * L * Y, X), f32),
            pltpu.VMEM((STEPS, N, 2, L // 2, SP, X), bf16),
            pltpu.VMEM((STEPS, N, 2, L // 2, SP, X), bf16),
            pltpu.VMEM((STEPS, N, 2, L // 2, SP, X), bf16),
            pltpu.VMEM((STEPS, Y, 2, E // 2, SP, X), bf16),
            pltpu.VMEM((STEPS, 2, SUB, X), f32),
            pltpu.VMEM((STEPS, Y, 4, SUB, X), f32),
            pltpu.VMEM((E, Y, X), jnp.int32),
            pltpu.VMEM((E, Y, X), f32),
            pltpu.VMEM((E, 32, X), f32),
            pltpu.VMEM(rep, f32),
            pltpu.VMEM(rep, f32),
            pltpu.VMEM((Y + 1, E, 8, X), f32),
            pltpu.VMEM(rep, f32),
            pltpu.VMEM(rep, f32),
            pltpu.VMEM(rep, f32),
            pltpu.VMEM(big, f32),
            pltpu.VMEM((M, S, X), f32),
            pltpu.VMEM((S, X), f32),
            pltpu.VMEM((S, X), f32),
            pltpu.VMEM((S, X), f32),
            pltpu.VMEM((2 * M, S), f32),
            pltpu.VMEM((L, X), f32),
            pltpu.VMEM(big, f32),
            pltpu.VMEM(big, f32),
            *[pltpu.VMEM((Y + 2, E, SP, X), f32)] * SUB,
            pltpu.VMEM((L * Y * SP, X), f32),
            dma((STEPS, 3, N)), dma((STEPS, 3, N)),
            dma((STEPS, 3, N)), dma((STEPS, 3, N)),
            dma((STEPS, 2, N)), dma((STEPS, 2, N)),
            dma((STEPS, 3, Y)), dma((STEPS, 3, Y)),
            dma((STEPS, 2)), dma((STEPS, 2)),
            dma((4,)), dma((4,)),
        ],
        compiler_params=pltpu.CompilerParams(
            collective_id=0, has_side_effects=True, vmem_limit_bytes=64 * 2**20 - 65536
        ),
    )(
        concentration, inhibit, priming, produce, max_rate.reshape(1, S), half_saturation.reshape(1, S),
        exudate.reshape(1, S), sorption_capacity, sorption_affinity, tortuosity.reshape(1, M),
        diffusivity.reshape(1, SP), velocity, material, root_mask,
    )


def solution(mesh):
    in_specs = (
        P("spec", "slab", None, None),
        P(), P(), P(), P(), P(), P(), P(), P(), P(),
        P("spec"),
        P("slab", None, None),
        P("slab", None, None),
        P("slab", None, None),
    )
    out_specs = P("spec", "slab", None, None)
    return jax.shard_map(body, mesh=mesh, in_specs=in_specs, out_specs=out_specs, check_vma=False)
```

```python
import functools

import jax
import jax.numpy as jnp
from jax import lax
from jax.experimental import pallas as pl
from jax.experimental.pallas import tpu as pltpu
from jax.sharding import PartitionSpec as P

SUB = 4
STEPS = 2
N = 16
NSLAB = 16
SP = 16
L = 8
E = L + 2 * SUB
Y = 16
X = 128
S = 256
M = 8
MESH = pl.DeviceIdType.MESH
f32 = jnp.float32
bf16 = jnp.bfloat16


def column(row):
    n = row.shape[1]
    eye = lax.broadcasted_iota(jnp.int32, (n, n), 0) == lax.broadcasted_iota(jnp.int32, (n, n), 1)
    return jnp.sum(jnp.where(eye, jnp.broadcast_to(row, (n, n)), 0.0), axis=1, keepdims=True)


def kernel(
    c_hbm, inhibit_hbm, priming_hbm, produce_hbm, rate_hbm, half_hbm, exudate_hbm, capacity_hbm, affinity_hbm,
    tort_hbm, dif_hbm, vel_hbm, mat_hbm, root_hbm, out_ref,
    c_ref, inhibit_ref, priming_ref, produce_ref, rate_ref, half_ref, exudate_ref, capacity_ref, affinity_ref,
    tort_ref, dif_ref, root_ref, sem_in,
    c32, send_a, recv_a, send_b, ren, den_send, den,
    matx, velx, tpad, cxr, cxl, fy, diag, cz, vz, ratio, uptake, mr, hs, ex, aff, root_b,
    fld, share, mob0, mob1, mob2, mob3, outs,
    sem_as, sem_ar, sem_bs, sem_br, sem_ds, sem_dr, sem_hs, sem_hr, sem_gs, sem_gr, sem_cs, sem_cr,
):
    mob = (mob0, mob1, mob2, mob3)
    me = lax.axis_index("spec")
    slab = lax.axis_index("slab")
    below = lax.rem(slab + 1, NSLAB)
    above = lax.rem(slab + NSLAB - 1, NSLAB)

    own = pl.ds(SUB, L)
    loads = [
        pltpu.make_async_copy(src, dst, sem_in.at[i])
        for i, (src, dst) in enumerate((
            (c_hbm, c_ref), (mat_hbm, matx.at[own]), (vel_hbm, velx.at[own]), (tort_hbm, tort_ref),
            (capacity_hbm, capacity_ref), (affinity_hbm, affinity_ref), (rate_hbm, rate_ref), (half_hbm, half_ref),
            (exudate_hbm, exudate_ref), (dif_hbm, dif_ref), (root_hbm, root_ref), (inhibit_hbm, inhibit_ref),
            (priming_hbm, priming_ref), (produce_hbm, produce_ref),
        ))
    ]
    for cp in loads:
        cp.start()

    x, z = me // 4, lax.rem(me, 4)

    def at(dx, dz):
        return lax.rem(x + dx, 4) * 4 + lax.rem(z + dz, 4)

    far = (2, 1, 3, 0)
    partners = [at(dx, dz) for dx in far for dz in far if dx or dz]

    barrier = pltpu.get_barrier_semaphore()

    @pl.loop(1, N)
    def _(d):
        pl.semaphore_signal(barrier, inc=1, device_id={"spec": lax.rem(me + d, N)}, device_id_type=MESH)

    for t in (below, above):
        pl.semaphore_signal(barrier, inc=1, device_id={"slab": t}, device_id_type=MESH)

    loads[0].wait()

    @pl.loop(0, SP)
    def _(s):
        for l in range(L):
            c32[pl.ds(s * L * Y + l * Y, Y), :] = c_ref[s, l].astype(f32)

    @pl.loop(0, N)
    def _(t):
        for p in range(L // 2):
            v = [c32[pl.ds(l * Y + t, SP, stride=L * Y), :] for l in (2 * p, 2 * p + 1)]
            for h in range(2):
                pair = jnp.concatenate([v[0][8 * h : 8 * h + 8], v[1][8 * h : 8 * h + 8]], axis=0)
                send_a[0, t, h, p] = pair.astype(bf16)

    pl.semaphore_wait(barrier, N + 1)

    both = pl.ds(0, 2)
    parts_a = (((both, pl.ds(0, 2)), (both, pl.ds(2, 2))), ((pl.ds(0, 1), pl.ds(0, 4)), (pl.ds(1, 1), pl.ds(0, 2)), (pl.ds(1, 1), pl.ds(2, 2))))
    parts_b = ((both, 0), (pl.ds(0, 1), 1), (pl.ds(1, 1), 1))

    def copy_a(st, i, t, slot):
        hs, ps = parts_a[st][i]
        return pltpu.make_async_remote_copy(
            send_a.at[st, t, hs, ps], recv_a.at[st, slot, hs, ps], sem_as.at[st, i, t], sem_ar.at[st, i, slot],
            device_id={"spec": t}, device_id_type=MESH,
        )

    def copy_b(st, i, t, slot):
        hs, q = parts_b[i]
        return pltpu.make_async_remote_copy(
            send_b.at[st, t, hs, pl.ds(2 * q, 2)], ren.at[st, slot, hs, pl.ds(2 + 2 * q, 2)], sem_bs.at[st, i, t],
            sem_br.at[st, i, slot], device_id={"spec": t}, device_id_type=MESH,
        )

    def copy_d(st, q, slot, t, key):
        return pltpu.make_async_remote_copy(
            den.at[st, slot, 1 + q], den.at[st, slot, 1 + q], sem_ds.at[st, q, key], sem_dr.at[st, q, slot],
            device_id={"spec": t}, device_id_type=MESH,
        )

    def start_d(st, q, dz):
        for dx in (2, 1, 3):
            copy_d(st, q, at(0, dz), at(dx, 0), at(dx, dz)).start()

    def forward_d(st, q):
        for dz in (1, 3, 2):
            slot = at(0, dz)
            copy_d(st, q, slot, slot, slot).wait_recv()
            start_d(st, q, dz)

    def copy_h(st, i, y):
        hs, q = parts_b[i]
        return pltpu.make_async_remote_copy(
            ren.at[st, y, hs, pl.ds(2 + 2 * q, 2)], ren.at[st, y, hs, pl.ds(6 - 6 * q, 2)],
            sem_hs.at[st, i, y], sem_hr.at[st, i, y],
            device_id={"slab": below if q else above}, device_id_type=MESH,
        )

    def copy_g(st, q):
        return pltpu.make_async_remote_copy(
            den.at[st, :, 1 + q], den.at[st, :, 3 * (1 - q)], sem_gs.at[st, q], sem_gr.at[st, q],
            device_id={"slab": below if q else above}, device_id_type=MESH,
        )

    def copies_c():
        out = []
        for i, ref in enumerate((matx, velx)):
            out.append(pltpu.make_async_remote_copy(
                ref.at[pl.ds(L, SUB)], ref.at[pl.ds(0, SUB)], sem_cs.at[2 * i], sem_cr.at[2 * i],
                device_id={"slab": below}, device_id_type=MESH,
            ))
            out.append(pltpu.make_async_remote_copy(
                ref.at[pl.ds(SUB, SUB)], ref.at[pl.ds(L + SUB, SUB)], sem_cs.at[2 * i + 1], sem_cr.at[2 * i + 1],
                device_id={"slab": above}, device_id_type=MESH,
            ))
        return out

    def start_a(st, i):
        for t in partners:
            copy_a(st, i, t, me).start()

    start_a(0, 0)
    start_a(0, 1)

    for cp in loads[1:]:
        cp.wait()
    rims = copies_c()
    for cp in rims:
        cp.start()

    for i in range(2):
        rows = pl.ds(i * 128, 128)
        for ref, src in ((mr, rate_ref), (hs, half_ref), (ex, exudate_ref)):
            ref[rows, :] = jnp.broadcast_to(column(src[:, rows]), (128, X))
        for g in range(M):
            up = capacity_ref[g : g + 1, rows] * affinity_ref[g : g + 1, rows]
            uptake[g, rows, :] = jnp.broadcast_to(column(up), (128, X))
    a_hi = affinity_ref[...].astype(bf16)
    aff[0:M, :] = a_hi.astype(f32)
    aff[M : 2 * M, :] = affinity_ref[...] - a_hi.astype(f32)
    for l in range(L):
        root_b[l : l + 1, :] = root_ref[l, pl.ds(me, 1), :].astype(f32)
    dif = jnp.broadcast_to(column(dif_ref[...]), (SP, X))
    dif_h = (dif[0:8], dif[8:16])
    lane = lax.broadcasted_iota(jnp.int32, (Y, X), 1)
    zero_row = jnp.zeros((SP, X), f32)
    tpad[...] = jnp.zeros_like(tpad)
    for k in range(SUB):
        for e in range(E):
            mob[k][0, e] = zero_row
            mob[k][Y + 1, e] = zero_row

    for cp in rims:
        cp.wait_recv()

    def inside(e):
        layer = slab * L + e - SUB
        return jnp.where((layer >= 0) & (layer < NSLAB * L), 1.0, 0.0).astype(f32)

    torts = [jnp.broadcast_to(tort_ref[:, g : g + 1], (Y, X)) for g in range(M)]

    def tort_of(e):
        m = matx[e]
        t = jnp.zeros((Y, X), f32)
        for g in range(M):
            t = jnp.where(m == g, torts[g], t)
        return t * inside(e)

    @pl.loop(0, E)
    def _(e):
        t = tort_of(e)
        tpad[e, pl.ds(8, Y), :] = t

    @pl.loop(0, E)
    def _(e):
        t = tpad[e, pl.ds(8, Y), :]
        right = 0.5 * (t + jnp.where(lane == X - 1, 0.0, pltpu.roll(t, X - 1, 1)))
        left = 0.5 * (t + jnp.where(lane == 0, 0.0, pltpu.roll(t, 1, 1)))
        north = 0.5 * (t + tpad[e, pl.ds(7, Y), :])
        south = 0.5 * (t + tpad[e, pl.ds(9, Y), :])
        total = right + left + north + south
        right = jnp.where(lane == X - 1, 0.0, right)
        left = jnp.where(lane == 0, 0.0, left)
        nxt = tpad[jnp.minimum(e + 1, E - 1), pl.ds(8, Y), :]
        zface = 0.5 * (t + nxt)
        v = velx[e]
        for y in range(Y):
            for ref, val in ((cxr, right), (cxl, left), (diag, total), (cz, zface), (vz, v)):
                ref[y, e] = jnp.broadcast_to(val[y : y + 1], (8, X))
            fy[y, e] = jnp.broadcast_to(north[y : y + 1], (8, X))
        fy[Y, e] = jnp.broadcast_to(south[Y - 1 : Y], (8, X))

    ups = [uptake[g, pl.ds(pl.multiple_of(me * SP, SP), SP), :] for g in range(M)]

    @pl.loop(0, E)
    def _(e):
        m = matx[e]
        for y in range(Y):
            row = jnp.broadcast_to(m[y : y + 1], (SP, X))
            r = ups[0]
            for g in range(1, M):
                r = jnp.where(row == g, ups[g], r)
            ratio[y, e] = r

    def react(st, q):
        @pl.loop(q * SUB // 2, (q + 1) * SUB // 2)
        def _(p):
            def twice(a):
                return jnp.concatenate([a, a], axis=1)

            l0 = 2 * p
            pairs = recv_a[st, :, :, p].astype(f32).reshape(N, 2, 2, 8, X)
            dissolved = jnp.concatenate([pairs[:, :, i].reshape(S, X) for i in range(2)], axis=1)
            gathered = dissolved.astype(bf16)
            inhibition = jnp.dot(inhibit_ref[...], gathered, preferred_element_type=f32)
            boost = jnp.dot(priming_ref[...], gathered, preferred_element_type=f32)
            rate = twice(mr[...]) * (1.0 + boost) / (twice(hs[...]) + dissolved + inhibition)
            remaining = dissolved * jnp.exp(-rate)
            consumed = (dissolved - remaining).astype(bf16)
            roots = jnp.concatenate([root_b[pl.ds(l0, 1), :], root_b[pl.ds(l0 + 1, 1), :]], axis=1)
            reacted = (
                remaining
                + jnp.dot(produce_ref[...], consumed, preferred_element_type=f32)
                + twice(ex[...]) * jnp.broadcast_to(roots, (S, 2 * X))
            )
            renewed = reacted.astype(bf16)
            low = (reacted - renewed.astype(f32)).astype(bf16)
            a16 = aff[...].astype(bf16)
            s_hi = jnp.dot(a16, renewed, preferred_element_type=f32)
            s_lo = jnp.dot(a16, low, preferred_element_type=f32)
            sums = s_hi[0:M] + s_hi[M:] + s_lo[0:M]
            for i in range(2):
                cols = slice(i * X, (i + 1) * X)
                labels = matx[SUB + l0 + i, pl.ds(me, 1), :]
                hit = jnp.broadcast_to(labels, (M, X)) == lax.broadcasted_iota(jnp.int32, (M, X), 0)
                d = 1.0 + jnp.sum(jnp.where(hit, sums[:, cols], 0.0), axis=0, keepdims=True)
                den_send[st, q, pl.ds(l0 - q * SUB + i, 1), :] = d
            split = [reacted[:, i * X : (i + 1) * X].reshape(N, 2, 1, 8, X) for i in range(2)]
            send_b[st, :, :, p] = jnp.concatenate(split, axis=2).reshape(N, 2, SP, X).astype(bf16)

    def prep(st, h, pairs, rim):
        rows = pl.ds(8 * h, 8)

        @pl.loop(0, Y // 2)
        def _(j):
            vals = []
            for y in (2 * j, 2 * j + 1):
                for pair in pairs:
                    r2 = ren[st, y, h, pair].astype(f32)
                    for i in range(2):
                        e = 2 * pair + i
                        r = r2[8 * i : 8 * i + 8]
                        d = jnp.broadcast_to(den[st, y, e // SUB, e % SUB : e % SUB + 1, :], (8, X))
                        s = d / (d + ratio[y, e, rows, :])
                        if rim:
                            s = s * inside(e)
                        vals.append((y, e, r, s))
            for y, e, r, s in vals:
                fld[y, e, rows, :] = r
                share[y, e, rows, :] = s
                mob[0][y + 1, e, rows, :] = s * r

    def substep(k, h, spans, n, finish=None):
        hr = pl.ds(8 * h, 8)
        src = mob[k]

        @pl.loop(0, Y // n)
        def _(j):
            y0 = j * n
            for es in spans:
                a = es[0]
                cen = [src[y0 + 1 + i, a, hr, :] for i in range(n)]
                prev = [src[y0 + 1 + i, a - 1, hr, :] for i in range(n)]
                fzp = [cz[y0 + i, a - 1] * (cen[i] - prev[i]) for i in range(n)]
                wp = [vz[y0 + i, a - 1] * prev[i] for i in range(n)]
                before = None
                for e in es:
                    rows = [src[y0, e, hr, :]] + cen + [src[y0 + n + 1, e, hr, :]]
                    fyv = [fy[y0 + i, e] for i in range(n + 1)]
                    nxt = [src[y0 + 1 + i, e + 1, hr, :] for i in range(n)]
                    done = []
                    for i in range(n):
                        y, m = y0 + i, cen[i]
                        fz = cz[y, e] * (nxt[i] - m)
                        w = vz[y, e] * m
                        acc = fz - fzp[i]
                        acc += cxr[y, e] * pltpu.roll(m, X - 1, 1) + cxl[y, e] * pltpu.roll(m, 1, 1)
                        acc += fyv[i] * rows[i] + fyv[i + 1] * rows[i + 2]
                        acc -= diag[y, e] * m
                        f = fld[y, e, hr, :] + (wp[i] - w) + dif_h[h] * acc
                        fzp[i], wp[i] = fz, w
                        if finish is None:
                            fld[y, e, hr, :] = f
                            mob[k + 1][y + 1, e, hr, :] = share[y, e, hr, :] * f
                        else:
                            done.append(f)
                    cen = nxt
                    if finish is not None:
                        if e % 2:
                            for i in range(n):
                                finish(y0 + i, e - 1 - SUB, before[i], done[i])
                        before = done

    def own_part(st, h):
        prep(st, h, range(2, 6), False)
        for k in range(SUB - 1):
            substep(k, h, [range(SUB + 1 + k, SUB + L - 1 - k)], (8, 16, 16)[k])

    def rest(st, h):
        prep(st, h, (0, 1, 6, 7), True)
        for k in range(SUB - 1):
            substep(k, h, [range(k + 1, SUB + 1 + k), range(SUB + L - 1 - k, E - 1 - k)], 8)

        def finish(y, l, f0, f1):
            if st < STEPS - 1:
                send_a[st + 1, y, h, l // 2] = jnp.concatenate([f0, f1], axis=0).astype(bf16)
            else:
                for i, f in enumerate((f0, f1)):
                    outs[pl.ds(pl.multiple_of((l + i) * Y * SP + y * SP + 8 * h, 8), 8), :] = f

        for q in range(2):
            substep(SUB - 1, h, [range(SUB + q * SUB, SUB + (q + 1) * SUB)], 8, finish)
            if st < STEPS - 1 and (h or q):
                start_a(st + 1, h * (1 + q))

    for st in range(STEPS):
        recv_a[st, me] = send_a[st, me]
        for q in range(2):

            @pl.loop(1, N)
            def _(d):
                src = lax.rem(me + N - d, N)
                if st and q == 0:
                    copy_a(st, 0, src, src).wait_recv()
                copy_a(st, q + st, src, src).wait_recv()

            react(st, q)

            den[st, me, 1 + q] = den_send[st, q]
            if q:
                forward_d(st, 0)
            for dz in (2, 1, 3):
                t = at(0, dz)
                copy_d(st, q, me, t, t).start()
            start_d(st, q, 0)
            for t in partners:
                copy_b(st, q, t, me).start()
            ren[st, me, :, pl.ds(2 + 2 * q, 2)] = send_b[st, me, :, pl.ds(2 * q, 2)]
            copy_h(st, q, me).start()

        for t in partners:
            copy_b(st, 2, t, me).start()
        copy_h(st, 2, me).start()
        for q in range(2):

            @pl.loop(1, N)
            def _(d):
                src = lax.rem(me + N - d, N)
                copy_b(st, q, src, src).wait_recv()
                copy_h(st, q, src).start()

            if q == 0:
                forward_d(st, 1)

        for q in range(2):

            @pl.loop(4, N)
            def _(d):
                slot = lax.rem(x + d // 4, 4) * 4 + lax.rem(d, 4)
                copy_d(st, q, slot, slot, slot).wait_recv()

            copy_g(st, q).start()

        own_part(st, 0)

        @pl.loop(1, N)
        def _(d):
            src = lax.rem(me + N - d, N)
            copy_b(st, 2, src, src).wait_recv()
            copy_h(st, 2, src).start()

        own_part(st, 1)

        for q in range(2):
            copy_g(st, q).wait_recv()

            @pl.loop(0, Y)
            def _(y):
                copy_h(st, q, y).wait_recv()

        rest(st, 0)

        @pl.loop(0, Y)
        def _(y):
            copy_h(st, 2, y).wait_recv()

        rest(st, 1)

    @pl.loop(0, SP)
    def _(s):
        for l in range(L):
            out_ref[s, l] = outs[pl.ds(l * Y * SP + s, Y, stride=SP), :].astype(bf16)

    for cp in rims:
        cp.wait_send()
    for st in range(STEPS):

        @pl.loop(1, N)
        def _(d):
            t = lax.rem(me + d, N)
            for i in range(len(parts_a[st])):
                copy_a(st, i, t, me).wait_send()
            for i in range(3):
                copy_b(st, i, t, me).wait_send()
            for q in range(2):
                copy_d(st, q, t, t, t).wait_send()

        @pl.loop(0, Y)
        def _(y):
            for i in range(3):
                copy_h(st, i, y).wait_send()

        for q in range(2):
            copy_g(st, q).wait_send()


def body(
    concentration, inhibit, priming, produce, max_rate, half_saturation, exudate,
    sorption_capacity, sorption_affinity, tortuosity, diffusivity, velocity, material, root_mask,
):
    vmem = pl.BlockSpec(memory_space=pltpu.VMEM)
    dma = pltpu.SemaphoreType.DMA
    big = (Y, E, SP, X)
    rep = (Y, E, 8, X)
    return pl.pallas_call(
        kernel,
        out_shape=jax.ShapeDtypeStruct((SP, L, Y, X), bf16),
        in_specs=[pl.BlockSpec(memory_space=pltpu.HBM)] * 14,
        out_specs=vmem,
        scratch_shapes=[
            pltpu.VMEM((SP, L, Y, X), bf16),
            pltpu.VMEM((S, S), bf16), pltpu.VMEM((S, S), bf16), pltpu.VMEM((S, S), bf16),
            pltpu.VMEM((1, S), f32), pltpu.VMEM((1, S), f32), pltpu.VMEM((1, S), f32),
            pltpu.VMEM((M, S), f32), pltpu.VMEM((M, S), f32),
            pltpu.VMEM((1, M), f32), pltpu.VMEM((1, SP), f32),
            pltpu.VMEM((L, Y, X), jnp.int32),
            dma((14,)),
            pltpu.VMEM((SP * L * Y, X), f32),
            pltpu.VMEM((STEPS, N, 2, L // 2, SP, X), bf16),
            pltpu.VMEM((STEPS, N, 2, L // 2, SP, X), bf16),
            pltpu.VMEM((STEPS, N, 2, L // 2, SP, X), bf16),
            pltpu.VMEM((STEPS, Y, 2, E // 2, SP, X), bf16),
            pltpu.VMEM((STEPS, 2, SUB, X), f32),
            pltpu.VMEM((STEPS, Y, 4, SUB, X), f32),
            pltpu.VMEM((E, Y, X), jnp.int32),
            pltpu.VMEM((E, Y, X), f32),
            pltpu.VMEM((E, 32, X), f32),
            pltpu.VMEM(rep, f32),
            pltpu.VMEM(rep, f32),
            pltpu.VMEM((Y + 1, E, 8, X), f32),
            pltpu.VMEM(rep, f32),
            pltpu.VMEM(rep, f32),
            pltpu.VMEM(rep, f32),
            pltpu.VMEM(big, f32),
            pltpu.VMEM((M, S, X), f32),
            pltpu.VMEM((S, X), f32),
            pltpu.VMEM((S, X), f32),
            pltpu.VMEM((S, X), f32),
            pltpu.VMEM((2 * M, S), f32),
            pltpu.VMEM((L, X), f32),
            pltpu.VMEM(big, f32),
            pltpu.VMEM(big, f32),
            *[pltpu.VMEM((Y + 2, E, SP, X), f32)] * SUB,
            pltpu.VMEM((L * Y * SP, X), f32),
            dma((STEPS, 3, N)), dma((STEPS, 3, N)),
            dma((STEPS, 3, N)), dma((STEPS, 3, N)),
            dma((STEPS, 2, N)), dma((STEPS, 2, N)),
            dma((STEPS, 3, Y)), dma((STEPS, 3, Y)),
            dma((STEPS, 2)), dma((STEPS, 2)),
            dma((4,)), dma((4,)),
        ],
        compiler_params=pltpu.CompilerParams(
            collective_id=0, has_side_effects=True, vmem_limit_bytes=64 * 2**20 - 65536
        ),
    )(
        concentration, inhibit, priming, produce, max_rate.reshape(1, S), half_saturation.reshape(1, S),
        exudate.reshape(1, S), sorption_capacity, sorption_affinity, tortuosity.reshape(1, M),
        diffusivity.reshape(1, SP), velocity, material, root_mask,
    )


def solution(mesh):
    in_specs = (
        P("spec", "slab", None, None),
        P(), P(), P(), P(), P(), P(), P(), P(), P(),
        P("spec"),
        P("slab", None, None),
        P("slab", None, None),
        P("slab", None, None),
    )
    out_specs = P("spec", "slab", None, None)
    return jax.shard_map(body, mesh=mesh, in_specs=in_specs, out_specs=out_specs, check_vma=False)
```
